32 devices in a mesh: ops: 4 (over x, core), sec: 8 (over z, y).
Axes of the slice: x: 2, y: 2, z: 4, core: 2. Of those that a mesh axis runs over, the one named last changes fastest.
Arguments:
- wavefunction: float32 [8, 256, 1024], P('sec', 'ops'), may hold values from -8 to 8
- left_ops: float32 [4, 8, 256, 256], P('ops', 'sec'), may hold values from -0.375 to 0.375
- right_ops: float32 [4, 256, 256], P('ops'), may hold values from -0.375 to 0.375
- site_ops: float32 [4, 4, 4], P('ops'), may hold values from -3 to 3
- pattern: int32 [4, 8], P('ops', 'sec'), may hold values 0 or 1
- sector_sizes: int32 [8], P('sec'), may hold values from 1 to 256, 1536 in all
- owner: int32 [4], P('ops'), may hold values from 0 to 3
- slot: int32 [4], P('ops'), may hold values from 0 to 1
Outputs:
- basis: float32 [8, 256, 1024], P('sec', 'ops')
- complementary: float32 [4, 2, 256, 256], P('ops', None, 'sec')
The draws below stay inside these ranges and needn't reach their ends.
Inputs may be any that keep to these rules, and one draw needn't show every extreme that they name: `sector_sizes`: each sector has at least one live state; some sector has all 256.
All inputs are finite; a program needn't handle non-finite values. No bound on the sum of `pattern` or of `sector_sizes` on one device may be relied on, other than what follows from the above.
Results may differ from the reference program's by a relative error of at most 0.0003.
Values sent between devices are 32-bit elements; how exact they have to be, the bound alone decides.
A program may use at most 64 MiB of HBM per device.

```python
import math
import jax
import jax.numpy as jnp
import numpy as np
from jax import lax

M = 256
C = 256
SLOTS = 2
OPS = 4
SEC = 8
N_OPS = 4


def draw_wavefunction(key, part):
    key_base = jax.random.fold_in(key, 11)
    key_sign = jax.random.fold_in(key, 12)
    key_common = jax.random.fold_in(key, 13)
    base_field = jax.random.normal(key_base, (SEC, M, 4 * C), jnp.float32)
    row_signs = jnp.where(jax.random.bernoulli(key_sign, 0.5, (SEC, M, 1)), 1.0, -1.0).astype(jnp.float32)
    common_row = jax.random.normal(key_common, (1, 1, 4 * C), jnp.float32)
    return jnp.clip(base_field + row_signs * common_row, -8.0, 8.0).astype(jnp.float32)


def set_ends(array, stream_key, low, high):
    index_at = [jax.random.randint(jax.random.fold_in(stream_key, axis), (), 0, length) for axis, length in enumerate(array.shape)]
    main_axis = array.shape.index(max(array.shape))
    neighbour = index_at[:main_axis] + [(index_at[main_axis] + 1) % array.shape[main_axis]] + index_at[main_axis + 1:]
    return array.at[tuple(index_at)].set(low).at[tuple(neighbour)].set(high)


def block_scale(stream_key, shape, shards, least, high):
    def one(position, parts):
        heights = jax.random.uniform(jax.random.fold_in(jax.random.fold_in(stream_key, 6), position), (parts,), jnp.float32, least / len(shards), high / len(shards))
        return jnp.repeat(jnp.exp(heights), shape[position] // parts).reshape((-1,) + (1,) * (len(shape) - position - 1))

    factor_of = one(*shards[0])
    for cut in shards[1:]:
        factor_of = factor_of * one(*cut)
    return factor_of


def rank_bounds(count, skew):
    weights = [(1 << 20) // math.isqrt(rank ** skew) + 1 for rank in range(1, count + 1)]
    scale = 1 + sum(weights) // (1 << 30)
    return np.cumsum(np.array([max(1, weight // scale) for weight in weights]))


def ranked(own_key, dims, count, slope):
    grid = rank_bounds(count, slope)
    pick = jax.random.randint(jax.random.fold_in(own_key, 1), dims, 0, int(grid[count - 1]))
    grade = jnp.searchsorted(jnp.asarray(grid, jnp.int32), pick, side="right")
    return jax.random.permutation(jax.random.fold_in(own_key, 2), count)[grade].astype(jnp.int32)


def length_profile(amount, total, limit, skew):
    loads = [(1 << 20) // math.isqrt(standing ** skew) + 1 for standing in range(2, amount + 1)]
    surplus, holding = total - limit - (amount - 1), [1] * (amount - 1)
    while surplus > 0:
        movable = [i for i in range(amount - 1) if holding[i] < limit]
        pool, budget = sum([loads[i] for i in movable]), surplus
        for i in movable:
            addition = min(limit - holding[i], max(1, budget * loads[i] // pool), surplus)
            holding[i] = holding[i] + addition
            surplus = surplus - addition
    return np.array([limit] + holding)


def ragged(own_key, number_of, total, limit, lean):
    if number_of == 2:
        one = jax.random.randint(own_key, (), max(1, total - limit), min(limit, total - 1) + 1)
        return jnp.stack([one, total - one])
    sizes = jnp.asarray(length_profile(number_of, total, limit, lean), jnp.int32)
    couples = (number_of - 1) // 2
    donor, sink = sizes[1:1 + 2 * couples:2], sizes[2:2 + 2 * couples:2]
    slack = jnp.minimum(donor - 1, limit - sink)
    passed = jax.random.randint(jax.random.fold_in(own_key, 1), (couples,), 0, 1 << 20) % (slack + 1)
    sizes = sizes.at[1:1 + 2 * couples:2].set(donor - passed).at[2:2 + 2 * couples:2].set(sink + passed)
    return sizes[jax.random.permutation(jax.random.fold_in(own_key, 2), number_of)]


def centred(stream_key, extent, deviation, bound, shards=(), kind=jnp.bfloat16):
    level = block_scale(stream_key, extent, shards, -0.22, 0.18) if shards else 1.0
    array = jax.random.normal(stream_key, extent, jnp.float32) * deviation * level
    return jnp.minimum(jnp.maximum(array, -bound), bound).astype(kind)


def setup_inputs(seed: int = 0) -> dict:
    key_list = jax.random.split(jax.random.key(seed), 9)
    wavefunction = draw_wavefunction(jax.random.fold_in(key_list[8], 71), 0)
    left_ops = centred(key_list[1], (OPS, SEC, M, M), M ** -0.5, 0.375, ((0, 4), (1, 8)), jnp.float32)
    right_ops = centred(key_list[2], (OPS, C, C), C ** -0.5, 0.375, ((0, 4),), jnp.float32)
    site_ops = centred(key_list[3], (OPS, 4, 4), 4 ** -0.5, 3.0, ((0, 4),), jnp.float32)
    pattern = set_ends((jax.random.randint(key_list[4], (OPS, SEC), 0, 4) < 3).astype(jnp.int32), jax.random.fold_in(key_list[4], 1), 0, 1)
    sector_sizes = ragged(key_list[5], SEC, SEC * M * 3 // 4, M, 2).astype(jnp.int32)
    owner = set_ends(ranked(key_list[6], (OPS,), N_OPS, 2), jax.random.fold_in(key_list[6], 3), 0, N_OPS - 1).astype(jnp.int32)
    slot = set_ends(jax.random.randint(key_list[7], (OPS,), 0, SLOTS), jax.random.fold_in(key_list[7], 1), 0, SLOTS - 1).astype(jnp.int32)
    return {"wavefunction": wavefunction, "left_ops": left_ops, "right_ops": right_ops, "site_ops": site_ops, "pattern": pattern, "sector_sizes": sector_sizes, "owner": owner, "slot": slot}


highest = lax.Precision.HIGHEST

def reference(wavefunction, left_ops, right_ops, site_ops, pattern, sector_sizes, owner, slot):
    sectors = wavefunction.shape[0]
    states = wavefunction.shape[1]
    columns = wavefunction.shape[2] // 4
    livemask = (jnp.arange(states, dtype=jnp.int32)[None, :] < sector_sizes[:, None]).astype(jnp.float32)
    source = (wavefunction * livemask[:, :, None]).reshape(sectors, states, 4, columns)
    blocks = left_ops * pattern[:, :, None, None].astype(jnp.float32)

    def apply_pair(accum, inputs):
        block, right, site = inputs
        mapped = jnp.einsum('smqc,cd->smqd', source, right, precision=highest)
        mapped = jnp.einsum('pq,smqd->smpd', site, mapped, precision=highest)
        return (accum + jnp.einsum('smn,snpd->smpd', block, mapped, precision=highest), None)
    start_value = jnp.zeros((sectors, states, 4, columns), jnp.float32)
    sigma, unused = lax.scan(apply_pair, start_value, (blocks, right_ops, site_ops))
    sigma = sigma * livemask[:, :, None, None]
    flat = sigma.reshape(sectors * states * 4, columns)
    gram = jnp.dot(flat.T.astype(jnp.float32), flat.astype(jnp.float32), precision=highest, preferred_element_type=jnp.float32)
    factor = jnp.linalg.cholesky(gram)
    ortho = jax.scipy.linalg.solve_triangular(factor, flat.T, lower=True).T
    scale = jnp.sqrt(jnp.float32(flat.shape[0]))
    basis = (ortho * scale).reshape(sectors, states, 4 * columns)
    frame = ortho.reshape(sectors, states, 4, columns)

    def renormalize(carry, inputs):
        block, site = inputs
        moved = jnp.einsum('smn,snqd->smqd', block, frame, precision=highest)
        moved = jnp.einsum('pq,smqd->smpd', site, moved, precision=highest)
        return (carry, jnp.einsum('smpc,smpd->cd', frame, moved, precision=highest))
    unused_carry, renorm = lax.scan(renormalize, jnp.zeros((), jnp.float32), (blocks, site_ops))
    target = owner * SLOTS + slot
    select = (target[:, None] == jnp.arange(N_OPS * SLOTS, dtype=jnp.int32)[None, :]).astype(jnp.float32)
    complementary = jnp.einsum('kj,kcd->jcd', select, renorm, precision=highest)
    return (basis, complementary.reshape(N_OPS, SLOTS, columns, columns))
```

```python
import functools

import jax
import jax.numpy as jnp
from jax import lax
from jax.experimental import pallas as pl
from jax.experimental.pallas import tpu as pltpu
from jax.sharding import PartitionSpec as P

SLOTS = 2
SITE = 4
HIGHEST = lax.Precision.HIGHEST
HIGH = lax.Precision.HIGH
MESH = pl.DeviceIdType.MESH
VM = pl.BlockSpec(memory_space=pltpu.VMEM)
SM = pl.BlockSpec(memory_space=pltpu.SMEM)
LIMIT = 40 * 1024 * 1024


def remote(src, dst, send, recv, dev):
    return pltpu.make_async_remote_copy(
        src_ref=src, dst_ref=dst, send_sem=send, recv_sem=recv, device_id=dev, device_id_type=MESH
    )


def greet(devs):
    barrier = pltpu.get_barrier_semaphore()
    for dev in devs:
        pl.semaphore_signal(barrier, inc=1, device_id=dev, device_id_type=MESH)
    pl.semaphore_wait(barrier, len(devs))


def dot(a, b, dims, precision):
    return lax.dot_general(a, b, (dims, ((), ())), precision=precision, preferred_element_type=jnp.float32)


NN = ((1,), (0,))
NT = ((1,), (1,))
TN = ((0,), (0,))


def gather_kernel(n, count, *refs):
    ins, outs = refs[:count], refs[count:2 * count]
    send, recv, local = refs[2 * count:]
    me = lax.axis_index("ops")
    chips = n // 2
    core = lax.rem(me, 2)
    chip = me // 2
    mate = {"ops": chip * 2 + 1 - core}
    away = [{"ops": lax.rem(chip + d, chips) * 2 + core} for d in range(1, chips)]
    back = [lax.rem(chip + chips - d, chips) * 2 + core for d in range(1, chips)]
    greet(away + [mate])
    direct = chips - 1
    started = []
    for a in range(count):
        for i, dev in enumerate(away):
            c = remote(ins[a], outs[a].at[me], send.at[a, i], recv.at[a, i], dev)
            c.start()
            started.append(c)
        c = remote(ins[a], outs[a].at[me], send.at[a, direct], recv.at[a, direct], mate)
        c.start()
        started.append(c)
    own = [pltpu.make_async_copy(ins[a], outs[a].at[me], local.at[a]) for a in range(count)]
    for c in own:
        c.start()
    relays = []
    for a in range(count):
        for i, src in enumerate(back):
            remote(ins[a], outs[a].at[src], send.at[a, i], recv.at[a, i], away[i]).wait_recv()
            c = remote(outs[a].at[src], outs[a].at[src], send.at[a, chips + i], recv.at[a, chips + i], mate)
            c.start()
            relays.append(c)
    for c in own:
        c.wait()
    for a in range(count):
        remote(ins[a], outs[a].at[me], send.at[a, direct], recv.at[a, direct], mate).wait_recv()
    for c in relays:
        c.wait_recv()
    for c in started + relays:
        c.wait_send()


def gather(n, arrays):
    count = len(arrays)
    return pl.pallas_call(
        functools.partial(gather_kernel, n, count),
        out_shape=[jax.ShapeDtypeStruct((n,) + a.shape, a.dtype) for a in arrays],
        in_specs=[VM] * count,
        out_specs=[VM] * count,
        scratch_shapes=[
            pltpu.SemaphoreType.DMA((count, n)),
            pltpu.SemaphoreType.DMA((count, n)),
            pltpu.SemaphoreType.DMA((count,)),
        ],
        compiler_params=pltpu.CompilerParams(collective_id=0, has_side_effects=True, vmem_limit_bytes=LIMIT),
    )(*arrays)


def sigma_kernel(size_ref, meta_ref, psi_ref, left_ref, right_ref, x_ref, gram_ref, mixed):
    rows, width = psi_ref.shape
    cols = width // SITE
    live = lax.broadcasted_iota(jnp.int32, (rows, cols), 0) < size_ref[0]
    total = jnp.zeros((rows, width), jnp.float32)
    for k in range(left_ref.shape[0]):
        mapped = [
            dot(jnp.where(live, psi_ref[:, q * cols:(q + 1) * cols], 0.0), right_ref[k], NN, HIGH)
            for q in range(SITE)
        ]
        for p in range(SITE):
            mix = mapped[0] * meta_ref[k, p * SITE]
            for q in range(1, SITE):
                mix += mapped[q] * meta_ref[k, p * SITE + q]
            mixed[:, p * cols:(p + 1) * cols] = mix
        total += dot(left_ref[k] * meta_ref[k, SITE * SITE], mixed[...], NN, HIGH)
    gram = jnp.zeros((cols, cols), jnp.float32)
    for p in range(SITE):
        part = jnp.where(live, total[:, p * cols:(p + 1) * cols], 0.0)
        x_ref[:, p * cols:(p + 1) * cols] = part
        gram += dot(part, part, TN, HIGHEST)
    gram_ref[...] = gram


def reduce_kernel(n, m, wide, gram_ref, out_ref, held, send, recv, send2, recv2):
    o, s = lax.axis_index("ops"), lax.axis_index("sec")
    size = gram_ref.shape[0]
    rows = held.shape[1]
    others = [(a, b) for a in range(n if wide else 1) for b in range(m) if a or b]
    devs = [{"ops": lax.rem(o + a, n), "sec": lax.rem(s + b, m)} for a, b in others]

    def place(a, b):
        at = a * m + b if wide else b
        return pl.ds(pl.multiple_of(at * rows, rows), rows)

    greet(devs)
    first = []
    for b in range(1, m):
        to = lax.rem(s + b, m)
        c = remote(gram_ref.at[place(o, to)], held.at[b - 1], send.at[b - 1], recv.at[b - 1], {"sec": to})
        c.start()
        first.append(c)
    mine = place(o, s)
    total = gram_ref[mine, :]
    for b in range(1, m):
        first[b - 1].wait_recv()
        total += held[b - 1]
    out_ref[mine, :] = total
    second = []
    for i, dev in enumerate(devs):
        c = remote(out_ref.at[mine], out_ref.at[mine], send2.at[i], recv2.at[i], dev)
        c.start()
        second.append(c)
    for i, (a, b) in enumerate(others):
        at = place(lax.rem(o + n - a, n), lax.rem(s + m - b, m))
        remote(out_ref.at[at], out_ref.at[at], send2.at[i], recv2.at[i], devs[i]).wait_recv()
    for c in first + second:
        c.wait_send()


def reduce_gram(n, m, gram):
    size = gram.shape[0]
    wide = size % (8 * n * m) == 0
    rows = size // (n * m) if wide else size // m
    peers = (n if wide else 1) * m - 1
    return pl.pallas_call(
        functools.partial(reduce_kernel, n, m, wide),
        out_shape=jax.ShapeDtypeStruct(gram.shape, jnp.float32),
        in_specs=[VM],
        out_specs=VM,
        scratch_shapes=[
            pltpu.VMEM((m - 1, rows, size), jnp.float32),
            pltpu.SemaphoreType.DMA((m - 1,)),
            pltpu.SemaphoreType.DMA((m - 1,)),
            pltpu.SemaphoreType.DMA((peers,)),
            pltpu.SemaphoreType.DMA((peers,)),
        ],
        compiler_params=pltpu.CompilerParams(collective_id=1, has_side_effects=True, vmem_limit_bytes=LIMIT),
    )(gram)


def small_inverse(block):
    b = block.shape[0]
    eye = (
        lax.broadcasted_iota(jnp.int32, (b, b), 0) == lax.broadcasted_iota(jnp.int32, (b, b), 1)
    ).astype(jnp.float32)
    work = jnp.concatenate([block, eye], axis=1)
    parts = [work[t * 8:(t + 1) * 8] for t in range(b // 8)]
    under = lax.broadcasted_iota(jnp.int32, (8, 1), 0)
    for j in range(b):
        t0, r = divmod(j, 8)
        row = parts[t0][r:r + 1, :]
        ratio = row / row[:, j:j + 1]
        for t in range(t0, b // 8):
            col = parts[t][:, j:j + 1]
            if t == t0:
                if r == 7:
                    continue
                col = jnp.where(under > r, col, 0.0)
            parts[t] = parts[t] - col * ratio
    work = jnp.concatenate(parts, axis=0)
    pivot = jnp.sum(work[:, :b] * eye, axis=1, keepdims=True)
    return work[:, b:] / jnp.sqrt(pivot)


def finish_kernel(scale, site_ref, gram_ref, x_ref, left_ref, basis_ref, renorm_ref, work, inverse, frame, mixed):
    cols = gram_ref.shape[0]
    rows = basis_ref.shape[0]
    block = 64
    work[:, :cols] = gram_ref[...]
    work[:, cols:] = (
        lax.broadcasted_iota(jnp.int32, (cols, cols), 0) == lax.broadcasted_iota(jnp.int32, (cols, cols), 1)
    ).astype(jnp.float32)
    for at in range(0, cols, block):
        end = at + block
        small = small_inverse(work[at:end, at:end])
        strip = dot(small, work[at:end, :], NN, HIGHEST)
        inverse[at:end, :] = strip[:, cols:]
        if end < cols:
            work[end:, :] -= dot(strip[:, end:cols], strip, TN, HIGHEST)
    for p in range(SITE):
        part = slice(p * cols, (p + 1) * cols)
        frame[:, part] = dot(x_ref[:, part], inverse[...], NT, HIGH)
    start = pl.multiple_of(lax.axis_index("ops") * rows, rows)
    basis_ref[...] = frame[pl.ds(start, rows), :] * scale
    for k in range(left_ref.shape[0]):
        mixed[...] = dot(left_ref[k] * site_ref[k, SITE * SITE], frame[...], NN, HIGH)
        moved = [mixed[:, q * cols:(q + 1) * cols] for q in range(SITE)]
        total = jnp.zeros((cols, cols), jnp.float32)
        for p in range(SITE):
            mix = moved[0] * site_ref[k, p * SITE]
            for q in range(1, SITE):
                mix += moved[q] * site_ref[k, p * SITE + q]
            total += dot(frame[:, p * cols:(p + 1) * cols], mix, TN, HIGH)
        renorm_ref[k] = total


def route_kernel(n, m, weight_ref, renorm_ref, out_ref, held, summed, send, recv, send2, recv2):
    o, s = lax.axis_index("ops"), lax.axis_index("sec")
    pairs, size, width = renorm_ref.shape
    rows = held.shape[2]
    secs = [{"sec": lax.rem(s + b, m)} for b in range(1, m)]
    opses = [{"ops": lax.rem(o + a, n)} for a in range(1, n)]
    greet(secs + opses)

    def place(b):
        return pl.ds(pl.multiple_of(b * rows, rows), rows)

    first = []
    for b in range(1, m):
        to = lax.rem(s + b, m)
        c = remote(renorm_ref.at[:, place(to)], held.at[b - 1], send.at[b - 1], recv.at[b - 1], {"sec": to})
        c.start()
        first.append(c)
    total = renorm_ref[:, place(s), :]
    for b in range(1, m):
        first[b - 1].wait_recv()
        total += held[b - 1]
    summed[0] = total
    second = []
    for a in range(1, n):
        c = remote(summed.at[0], summed.at[a], send2.at[a - 1], recv2.at[a - 1], opses[a - 1])
        c.start()
        second.append(c)
    out = [jnp.zeros((rows, width), jnp.float32) for _ in range(SLOTS)]
    for a in range(n):
        if a:
            second[a - 1].wait_recv()
        for k in range(pairs):
            term = summed[a, k]
            for j in range(SLOTS):
                out[j] += term * weight_ref[a * pairs + k, j]
    for j in range(SLOTS):
        out_ref[j] = out[j]
    for c in first + second:
        c.wait_send()


def body(n, m, wavefunction, left_ops, right_ops, site_ops, pattern, sector_sizes, owner, slot):
    row_share, width = wavefunction.shape[1:]
    pairs = left_ops.shape[0]
    cols = width // SITE
    states = row_share * n
    f32 = jnp.float32
    meta = jnp.concatenate(
        [
            site_ops.reshape(pairs, SITE * SITE),
            pattern[:, :1].astype(f32),
            owner[:, None].astype(f32),
            slot[:, None].astype(f32),
        ],
        axis=1,
    )
    meta = jnp.pad(meta, ((0, 0), (0, 128 - meta.shape[1])))
    left = left_ops[:, 0]
    psi, left_all, right_all, meta_all = gather(n, [wavefunction[0], left, right_ops, meta])
    meta_all = meta_all.reshape(n * pairs, 128)
    x, gram = pl.pallas_call(
        sigma_kernel,
        out_shape=[jax.ShapeDtypeStruct((states, width), f32), jax.ShapeDtypeStruct((cols, cols), f32)],
        in_specs=[SM, SM, VM, VM, VM],
        out_specs=[VM, VM],
        scratch_shapes=[pltpu.VMEM((states, width), f32)],
        compiler_params=pltpu.CompilerParams(vmem_limit_bytes=LIMIT),
    )(
        sector_sizes,
        meta_all[:, :SITE * SITE + 1],
        psi.reshape(states, width),
        left_all.reshape(n * pairs, states, states),
        right_all.reshape(n * pairs, cols, cols),
    )
    gram = reduce_gram(n, m, gram)
    scale = float(SITE * states * m) ** 0.5
    basis, renorm = pl.pallas_call(
        functools.partial(finish_kernel, scale),
        out_shape=[
            jax.ShapeDtypeStruct((row_share, width), f32),
            jax.ShapeDtypeStruct((pairs, cols, cols), f32),
        ],
        in_specs=[SM, VM, VM, VM],
        out_specs=[VM, VM],
        scratch_shapes=[
            pltpu.VMEM((cols, 2 * cols), f32),
            pltpu.VMEM((cols, cols), f32),
            pltpu.VMEM((states, width), f32),
            pltpu.VMEM((states, width), f32),
        ],
        compiler_params=pltpu.CompilerParams(vmem_limit_bytes=LIMIT),
    )(meta[:, :SITE * SITE + 1], gram, x, left)
    me = lax.axis_index("ops")
    order = (me - jnp.arange(n, dtype=jnp.int32) + n) % n
    facts = meta_all.reshape(n, pairs, 128)[order].reshape(n * pairs, 128)[:, SITE * SITE + 1:SITE * SITE + 3]
    target = facts[:, 0] * SLOTS + facts[:, 1] - (me * SLOTS).astype(f32)
    weight = (target[:, None] == jnp.arange(SLOTS, dtype=f32)[None, :]).astype(f32)
    rows = cols // m
    complementary = pl.pallas_call(
        functools.partial(route_kernel, n, m),
        out_shape=jax.ShapeDtypeStruct((SLOTS, rows, cols), f32),
        in_specs=[SM, VM],
        out_specs=VM,
        scratch_shapes=[
            pltpu.VMEM((m - 1, pairs, rows, cols), f32),
            pltpu.VMEM((n, pairs, rows, cols), f32),
            pltpu.SemaphoreType.DMA((m - 1,)),
            pltpu.SemaphoreType.DMA((m - 1,)),
            pltpu.SemaphoreType.DMA((n - 1,)),
            pltpu.SemaphoreType.DMA((n - 1,)),
        ],
        compiler_params=pltpu.CompilerParams(collective_id=2, has_side_effects=True, vmem_limit_bytes=LIMIT),
    )(weight, renorm)
    return basis[None], complementary[None]


def solution(mesh):
    placed = (
        P("sec", "ops", None),
        P("ops", "sec", None, None),
        P("ops", None, None),
        P("ops", None, None),
        P("ops", "sec"),
        P("sec"),
        P("ops"),
        P("ops"),
    )
    return jax.shard_map(
        functools.partial(body, mesh.shape["ops"], mesh.shape["sec"]),
        mesh=mesh,
        in_specs=placed,
        out_specs=(P("sec", "ops", None), P("ops", None, "sec", None)),
        check_vma=False,
    )
```

```python
import functools

import jax
import jax.numpy as jnp
from jax import lax
from jax.experimental import pallas as pl
from jax.experimental.pallas import tpu as pltpu
from jax.sharding import PartitionSpec as P

SLOTS = 2
SITE = 4
HIGHEST = lax.Precision.HIGHEST
HIGH = lax.Precision.HIGH
MESH = pl.DeviceIdType.MESH
VM = pl.BlockSpec(memory_space=pltpu.VMEM)
SM = pl.BlockSpec(memory_space=pltpu.SMEM)
ANY = pl.BlockSpec(memory_space=pl.ANY)
LIMIT = 48 * 1024 * 1024


def remote(src, dst, send, recv, dev):
    return pltpu.make_async_remote_copy(
        src_ref=src, dst_ref=dst, send_sem=send, recv_sem=recv, device_id=dev, device_id_type=MESH
    )


def greet(devs):
    barrier = pltpu.get_barrier_semaphore()
    for dev in devs:
        pl.semaphore_signal(barrier, inc=1, device_id=dev, device_id_type=MESH)
    pl.semaphore_wait(barrier, len(devs))


def dot(a, b, dims, precision):
    return lax.dot_general(a, b, (dims, ((), ())), precision=precision, preferred_element_type=jnp.float32)


NN = ((1,), (0,))
NT = ((1,), (1,))
TN = ((0,), (0,))


def small_inverse(block):
    b = block.shape[0]
    eye = (
        lax.broadcasted_iota(jnp.int32, (b, b), 0) == lax.broadcasted_iota(jnp.int32, (b, b), 1)
    ).astype(jnp.float32)
    work = jnp.concatenate([block, eye], axis=1)
    lanes = work.shape[1]
    count = b // 8
    parts = [work[t * 8:(t + 1) * 8] for t in range(count)]
    under = lax.broadcasted_iota(jnp.int32, (8, lanes), 0)
    for g in range(count):
        spread = [
            [jnp.broadcast_to(parts[t][:, g * 8 + i:g * 8 + i + 1], (8, lanes)) for i in range(8)]
            for t in range(g, count)
        ]
        rows = parts[g]
        for r in range(8):
            inv = 1.0 / spread[0][r][r:r + 1, :]
            ratio = rows[r:r + 1, :] * inv
            steps = [spread[0][i][r:r + 1, :] * inv for i in range(r + 1, 8)]
            for t in range(count - g):
                col = spread[t][r]
                if t == 0:
                    if r == 7:
                        continue
                    col = jnp.where(under > r, col, 0.0)
                    rows = rows - col * ratio
                else:
                    parts[g + t] = parts[g + t] - col * ratio
                for i in range(r + 1, 8):
                    spread[t][i] = spread[t][i] - col * steps[i - r - 1]
        parts[g] = rows
    work = jnp.concatenate(parts, axis=0)
    pivot = jnp.sum(work[:, :b] * eye, axis=1, keepdims=True)
    return work[:, b:] / jnp.sqrt(pivot)


def kernel(
    n, m, wide, scale, size_ref, meta_in, psi_in, left_in, right_in, basis_ref, out_ref,
    meta, psi, left, right, mixed, x, gram, whole, held, work, inverse, frame, renorm, taken, summed,
    send, recv, local, send1, recv1, send2, recv2, send3, recv3, send4, recv4,
):
    o, s = lax.axis_index("ops"), lax.axis_index("sec")
    pairs = left_in.shape[0]
    row_share, width = psi_in.shape
    states = row_share * n
    cols = width // SITE
    others = [(a, b) for a in range(n) for b in range(m) if (a or b) and (wide or not a or not b)]
    devs = [{"ops": lax.rem(o + a, n), "sec": lax.rem(s + b, m)} for a, b in others]
    greet(devs)

    ins, outs = (meta_in, psi_in, right_in, left_in), (meta, psi, right, left)
    chips = n // 2
    core = lax.rem(o, 2)
    chip = o // 2
    direct = chips - 1
    mate_at = chip * 2 + 1 - core
    mate = {"ops": mate_at, "sec": s}
    away = [{"ops": lax.rem(chip + d, chips) * 2 + core, "sec": s} for d in range(1, chips)]
    back = [lax.rem(chip + chips - d, chips) * 2 + core for d in range(1, chips)]
    far = [lax.rem(chip + chips - d, chips) * 2 + 1 - core for d in range(1, chips)]
    pending = []

    def begin(c):
        c.start()
        pending.append(c)
        return c

    own = [pltpu.make_async_copy(ins[a], outs[a].at[o], local.at[a]) for a in range(4)]
    for a in range(4):
        for i, dev in enumerate(away):
            begin(remote(ins[a], outs[a].at[o], send.at[a, i], recv.at[a, i], dev))
        begin(remote(ins[a], outs[a].at[o], send.at[a, direct], recv.at[a, direct], mate))
        own[a].start()

    def relay(a):
        for i, src in enumerate(back):
            remote(ins[a], outs[a].at[src], send.at[a, i], recv.at[a, i], away[i]).wait_recv()
            begin(remote(outs[a].at[src], outs[a].at[src], send.at[a, chips + i], recv.at[a, chips + i], mate))

    def from_mate(a):
        remote(ins[a], outs[a].at[mate_at], send.at[a, direct], recv.at[a, direct], mate).wait_recv()

    def from_far(a, i):
        remote(outs[a].at[far[i]], outs[a].at[far[i]], send.at[a, chips + i], recv.at[a, chips + i], mate).wait_recv()

    for a in (0, 1):
        own[a].wait()
        from_mate(a)
        relay(a)
        for i in range(direct):
            from_far(a, i)

    live = lax.broadcasted_iota(jnp.int32, (states, width), 0) < size_ref[0]
    x[...] = jnp.where(live, psi[...].reshape(states, width), 0.0)
    order = [o, mate_at] + back + far

    def scalar(at, k, i):
        return meta[at, k:k + 1, i:i + 1]

    def mix_site(parts, at, k, p):
        total = parts[0] * scalar(at, k, p * SITE)
        for q in range(1, SITE):
            total += parts[q] * scalar(at, k, p * SITE + q)
        return total

    def map_right(i):
        for k in range(pairs):
            mapped = [
                dot(x[:, q * cols:(q + 1) * cols], right[order[i], k], NN, HIGH) for q in range(SITE)
            ]
            for p in range(SITE):
                mixed[i * pairs + k, :, p * cols:(p + 1) * cols] = mix_site(mapped, order[i], k, p)

    def apply_left(i, total):
        for k in range(pairs):
            block = left[order[i], k] * scalar(order[i], k, SITE * SITE)
            total = total + dot(block, mixed[i * pairs + k], NN, HIGH)
        return total

    def arrive(a, i):
        if i == 0:
            own[a].wait()
        elif i == 1:
            from_mate(a)
        elif i < 2 + direct:
            if i == 2:
                relay(a)
        else:
            from_far(a, i - 2 - direct)

    for i in range(n):
        arrive(2, i)
        map_right(i)
    total = jnp.zeros((states, width), jnp.float32)
    for i in range(n):
        arrive(3, i)
        total = apply_left(i, total)
    x[...] = jnp.where(live, total, 0.0)
    gram[...] = sum(dot(x[:, p * cols:(p + 1) * cols], x[:, p * cols:(p + 1) * cols], TN, HIGHEST) for p in range(SITE))

    rows = held.shape[1]

    def place(a, b):
        at = a * m + b if wide else b
        return pl.ds(pl.multiple_of(at * rows, rows), rows)

    first = []
    for b in range(1, m):
        to = lax.rem(s + b, m)
        dev = {"ops": o, "sec": to}
        first.append(begin(remote(gram.at[place(o, to)], held.at[b - 1], send1.at[b - 1], recv1.at[b - 1], dev)))
    mine = place(o, s)
    part = gram[mine, :]
    for b in range(1, m):
        first[b - 1].wait_recv()
        part += held[b - 1]
    whole[mine, :] = part
    peers = [(i, a, b) for i, (a, b) in enumerate(others) if wide or not a]
    for i, a, b in peers:
        begin(remote(whole.at[mine], whole.at[mine], send2.at[i], recv2.at[i], devs[i]))
    for i, a, b in peers:
        at = place(lax.rem(o + n - a, n), lax.rem(s + m - b, m))
        remote(whole.at[at], whole.at[at], send2.at[i], recv2.at[i], devs[i]).wait_recv()

    block = 64
    work[:, :cols] = whole[...]
    work[:, cols:] = (
        lax.broadcasted_iota(jnp.int32, (cols, cols), 0) == lax.broadcasted_iota(jnp.int32, (cols, cols), 1)
    ).astype(jnp.float32)
    for at in range(0, cols, block):
        end = at + block
        small = small_inverse(work[at:end, at:end])
        strip = dot(small, work[at:end, :], NN, HIGHEST)
        inverse[at:end, :] = strip[:, cols:]
        if end < cols:
            work[end:, :] -= dot(strip[:, end:cols], strip, TN, HIGHEST)
    for p in range(SITE):
        part = slice(p * cols, (p + 1) * cols)
        frame[:, part] = dot(x[:, part], inverse[...], NT, HIGH)

    for k in range(pairs):
        moved = dot(left_in_block(left, o, k, scalar), frame[...], NN, HIGH)
        moved = [moved[:, q * cols:(q + 1) * cols] for q in range(SITE)]
        renorm[k] = sum(
            dot(frame[:, p * cols:(p + 1) * cols], mix_site(moved, o, k, p), TN, HIGH) for p in range(SITE)
        )
    share = taken.shape[2]

    def portion(b):
        return pl.ds(pl.multiple_of(b * share, share), share)

    third = []
    for b in range(1, m):
        to = lax.rem(s + b, m)
        dev = {"ops": o, "sec": to}
        third.append(begin(remote(renorm.at[:, portion(to)], taken.at[b - 1], send3.at[b - 1], recv3.at[b - 1], dev)))
    basis_ref[...] = frame[pl.ds(pl.multiple_of(o * row_share, row_share), row_share), :] * scale
    sector = renorm[:, portion(s), :]
    for b in range(1, m):
        third[b - 1].wait_recv()
        sector += taken[b - 1]
    summed[0] = sector
    fourth = []
    for a in range(1, n):
        dev = {"ops": lax.rem(o + a, n), "sec": s}
        fourth.append(begin(remote(summed.at[0], summed.at[a], send4.at[a - 1], recv4.at[a - 1], dev)))
    result = [jnp.zeros((share, cols), jnp.float32) for _ in range(SLOTS)]
    base = (o * SLOTS).astype(jnp.float32)
    for a in range(n):
        if a:
            fourth[a - 1].wait_recv()
        at = lax.rem(o + n - a, n)
        for k in range(pairs):
            term = summed[a, k]
            target = scalar(at, k, SITE * SITE + 1) * SLOTS + scalar(at, k, SITE * SITE + 2) - base
            for j in range(SLOTS):
                result[j] += term * (target == j).astype(jnp.float32)
    for j in range(SLOTS):
        out_ref[j] = result[j]
    for c in pending:
        c.wait_send()


def left_in_block(left, at, k, scalar):
    return left[at, k] * scalar(at, k, SITE * SITE)


def body(n, m, wavefunction, left_ops, right_ops, site_ops, pattern, sector_sizes, owner, slot):
    row_share, width = wavefunction.shape[1:]
    pairs = left_ops.shape[0]
    cols = width // SITE
    states = row_share * n
    f32 = jnp.float32
    meta = jnp.concatenate(
        [
            site_ops.reshape(pairs, SITE * SITE),
            pattern[:, :1].astype(f32),
            owner[:, None].astype(f32),
            slot[:, None].astype(f32),
        ],
        axis=1,
    )
    meta = jnp.pad(meta, ((0, 0), (0, 128 - meta.shape[1])))
    wide = cols % (8 * n * m) == 0
    rows = cols // (n * m) if wide else cols // m
    share = cols // m
    dma = pltpu.SemaphoreType.DMA
    peers = n * m - 1
    basis, complementary = pl.pallas_call(
        functools.partial(kernel, n, m, wide, float(SITE * states * m) ** 0.5),
        out_shape=[
            jax.ShapeDtypeStruct((row_share, width), f32),
            jax.ShapeDtypeStruct((SLOTS, share, cols), f32),
        ],
        in_specs=[SM, VM, ANY, ANY, ANY],
        out_specs=[VM, VM],
        scratch_shapes=[
            pltpu.VMEM((n, pairs, 128), f32),
            pltpu.VMEM((n, row_share, width), f32),
            pltpu.VMEM((n, pairs, states, states), f32),
            pltpu.VMEM((n, pairs, cols, cols), f32),
            pltpu.VMEM((n * pairs, states, width), f32),
            pltpu.VMEM((states, width), f32),
            pltpu.VMEM((cols, cols), f32),
            pltpu.VMEM((cols, cols), f32),
            pltpu.VMEM((m - 1, rows, cols), f32),
            pltpu.VMEM((cols, 2 * cols), f32),
            pltpu.VMEM((cols, cols), f32),
            pltpu.VMEM((states, width), f32),
            pltpu.VMEM((pairs, cols, cols), f32),
            pltpu.VMEM((m - 1, pairs, share, cols), f32),
            pltpu.VMEM((n, pairs, share, cols), f32),
            dma((4, n)),
            dma((4, n)),
            dma((4,)),
            dma((m - 1,)),
            dma((m - 1,)),
            dma((peers,)),
            dma((peers,)),
            dma((m - 1,)),
            dma((m - 1,)),
            dma((n - 1,)),
            dma((n - 1,)),
        ],
        compiler_params=pltpu.CompilerParams(collective_id=0, has_side_effects=True, vmem_limit_bytes=LIMIT),
    )(sector_sizes, meta, wavefunction[0], left_ops[:, 0], right_ops)
    return basis[None], complementary[None]


def solution(mesh):
    placed = (
        P("sec", "ops", None),
        P("ops", "sec", None, None),
        P("ops", None, None),
        P("ops", None, None),
        P("ops", "sec"),
        P("sec"),
        P("ops"),
        P("ops"),
    )
    return jax.shard_map(
        functools.partial(body, mesh.shape["ops"], mesh.shape["sec"]),
        mesh=mesh,
        in_specs=placed,
        out_specs=(P("sec", "ops", None), P("ops", None, "sec", None)),
        check_vma=False,
    )
```

```python
import functools

import jax
import jax.numpy as jnp
from jax import lax
from jax.experimental import pallas as pl
from jax.experimental.pallas import tpu as pltpu
from jax.sharding import PartitionSpec as P

SLOTS = 2
SITE = 4
HIGHEST = lax.Precision.HIGHEST
HIGH = lax.Precision.HIGH
MESH = pl.DeviceIdType.MESH
VM = pl.BlockSpec(memory_space=pltpu.VMEM)
SM = pl.BlockSpec(memory_space=pltpu.SMEM)
ANY = pl.BlockSpec(memory_space=pl.ANY)
LIMIT = 60 * 1024 * 1024


def remote(src, dst, send, recv, dev):
    return pltpu.make_async_remote_copy(
        src_ref=src, dst_ref=dst, send_sem=send, recv_sem=recv, device_id=dev, device_id_type=MESH
    )


def greet(devs):
    barrier = pltpu.get_barrier_semaphore()
    for dev in devs:
        pl.semaphore_signal(barrier, inc=1, device_id=dev, device_id_type=MESH)
    pl.semaphore_wait(barrier, len(devs))


def dot(a, b, dims, precision):
    return lax.dot_general(a, b, (dims, ((), ())), precision=precision, preferred_element_type=jnp.float32)


NN = ((1,), (0,))
NT = ((1,), (1,))
TN = ((0,), (0,))


def small_inverse(block):
    b = block.shape[0]
    eye = (
        lax.broadcasted_iota(jnp.int32, (b, b), 0) == lax.broadcasted_iota(jnp.int32, (b, b), 1)
    ).astype(jnp.float32)
    work = jnp.concatenate([block, eye], axis=1)
    lanes = work.shape[1]
    count = b // 8
    parts = [work[t * 8:(t + 1) * 8] for t in range(count)]
    under = lax.broadcasted_iota(jnp.int32, (8, lanes), 0)
    for g in range(count):
        spread = [
            [jnp.broadcast_to(parts[t][:, g * 8 + i:g * 8 + i + 1], (8, lanes)) for i in range(8)]
            for t in range(g, count)
        ]
        rows = parts[g]
        for r in range(8):
            inv = 1.0 / spread[0][r][r:r + 1, :]
            ratio = rows[r:r + 1, :] * inv
            steps = [spread[0][i][r:r + 1, :] * inv for i in range(r + 1, 8)]
            for t in range(count - g):
                col = spread[t][r]
                if t == 0:
                    if r == 7:
                        continue
                    col = jnp.where(under > r, col, 0.0)
                    rows = rows - col * ratio
                else:
                    parts[g + t] = parts[g + t] - col * ratio
                for i in range(r + 1, 8):
                    spread[t][i] = spread[t][i] - col * steps[i - r - 1]
        parts[g] = rows
    work = jnp.concatenate(parts, axis=0)
    pivot = jnp.sum(work[:, :b] * eye, axis=1, keepdims=True)
    return work[:, b:] / jnp.sqrt(pivot)


def kernel(
    n, m, wide, scale, size_ref, meta_in, psi_in, left_in, right_in, basis_ref, out_ref,
    meta, psi, left, right, mixed, x, gram, whole, held, work, inverse, frame, renorm, moved, merged, taken, summed,
    send, recv, local, send1, recv1, send2, recv2, send3, recv3, send4, recv4, send5, recv5,
):
    o, s = lax.axis_index("ops"), lax.axis_index("sec")
    pairs = left_in.shape[0]
    row_share, width = psi_in.shape
    states = row_share * n
    cols = width // SITE
    others = [(a, b) for a in range(n) for b in range(m) if (a or b) and (wide or not a or not b)]
    devs = [{"ops": lax.rem(o + a, n), "sec": lax.rem(s + b, m)} for a, b in others]
    greet(devs)

    ins, outs = (meta_in, psi_in, right_in, left_in), (meta, psi, right, left)
    chips = n // 2
    core = lax.rem(o, 2)
    chip = o // 2
    direct = chips - 1
    mate_at = chip * 2 + 1 - core
    mate = {"ops": mate_at, "sec": s}
    away = [{"ops": lax.rem(chip + d, chips) * 2 + core, "sec": s} for d in range(1, chips)]
    back = [lax.rem(chip + chips - d, chips) * 2 + core for d in range(1, chips)]
    far = [lax.rem(chip + chips - d, chips) * 2 + 1 - core for d in range(1, chips)]
    pending = []

    def begin(c):
        c.start()
        pending.append(c)
        return c

    own = [pltpu.make_async_copy(ins[a], outs[a].at[o], local.at[a]) for a in range(4)]
    for a in range(4):
        for i, dev in enumerate(away):
            begin(remote(ins[a], outs[a].at[o], send.at[a, i], recv.at[a, i], dev))
        begin(remote(ins[a], outs[a].at[o], send.at[a, direct], recv.at[a, direct], mate))
        own[a].start()

    def relay(a):
        for i, src in enumerate(back):
            remote(ins[a], outs[a].at[src], send.at[a, i], recv.at[a, i], away[i]).wait_recv()
            begin(remote(outs[a].at[src], outs[a].at[src], send.at[a, chips + i], recv.at[a, chips + i], mate))

    def from_mate(a):
        remote(ins[a], outs[a].at[mate_at], send.at[a, direct], recv.at[a, direct], mate).wait_recv()

    def from_far(a, i):
        remote(outs[a].at[far[i]], outs[a].at[far[i]], send.at[a, chips + i], recv.at[a, chips + i], mate).wait_recv()

    for a in (0, 1):
        own[a].wait()
        from_mate(a)
        relay(a)
        for i in range(direct):
            from_far(a, i)

    live = lax.broadcasted_iota(jnp.int32, (states, width), 0) < size_ref[0]
    x[...] = jnp.where(live, psi[...].reshape(states, width), 0.0)
    order = [o, mate_at] + back + far

    def scalar(at, k, i):
        return meta[at, k:k + 1, i:i + 1]

    def mix_site(parts, at, k, p):
        total = parts[0] * scalar(at, k, p * SITE)
        for q in range(1, SITE):
            total += parts[q] * scalar(at, k, p * SITE + q)
        return total

    def map_right(i):
        for k in range(pairs):
            mapped = [
                dot(x[:, q * cols:(q + 1) * cols], right[order[i], k], NN, HIGH) for q in range(SITE)
            ]
            for p in range(SITE):
                mixed[i * pairs + k, :, p * cols:(p + 1) * cols] = mix_site(mapped, order[i], k, p)

    def apply_left(i, total):
        for k in range(pairs):
            block = left[order[i], k] * scalar(order[i], k, SITE * SITE)
            total = total + dot(block, mixed[i * pairs + k], NN, HIGH)
        return total

    def arrive(a, i):
        if i == 0:
            own[a].wait()
        elif i == 1:
            from_mate(a)
        elif i < 2 + direct:
            if i == 2:
                relay(a)
        else:
            from_far(a, i - 2 - direct)

    for i in range(n):
        arrive(2, i)
        map_right(i)
    total = jnp.zeros((states, width), jnp.float32)
    for i in range(n):
        arrive(3, i)
        total = apply_left(i, total)
    x[...] = jnp.where(live, total, 0.0)
    gram[...] = sum(dot(x[:, p * cols:(p + 1) * cols], x[:, p * cols:(p + 1) * cols], TN, HIGHEST) for p in range(SITE))

    rows = held.shape[1]

    def place(a, b):
        at = a * m + b if wide else b
        return pl.ds(pl.multiple_of(at * rows, rows), rows)

    first = []
    for b in range(1, m):
        to = lax.rem(s + b, m)
        dev = {"ops": o, "sec": to}
        first.append(begin(remote(gram.at[place(o, to)], held.at[b - 1], send1.at[b - 1], recv1.at[b - 1], dev)))
    for k in range(pairs):
        moved[k] = dot(left[o, k] * scalar(o, k, SITE * SITE), x[...], NN, HIGHEST)
    mine = place(o, s)
    part = gram[mine, :]
    for b in range(1, m):
        first[b - 1].wait_recv()
        part += held[b - 1]
    whole[mine, :] = part
    peers = [(i, a, b) for i, (a, b) in enumerate(others) if wide or not a]
    for i, a, b in peers:
        begin(remote(whole.at[mine], whole.at[mine], send2.at[i], recv2.at[i], devs[i]))
    for k in range(pairs):
        parts = [moved[k, :, q * cols:(q + 1) * cols] for q in range(SITE)]
        renorm[k] = sum(
            dot(x[:, p * cols:(p + 1) * cols], mix_site(parts, o, k, p), TN, HIGHEST) for p in range(SITE)
        )
    for i, a, b in peers:
        at = place(lax.rem(o + n - a, n), lax.rem(s + m - b, m))
        remote(whole.at[at], whole.at[at], send2.at[i], recv2.at[i], devs[i]).wait_recv()

    share = taken.shape[2]

    def portion(b):
        return pl.ds(pl.multiple_of(b * share, share), share)

    ours = portion(s)
    third = []
    for b in range(1, m):
        to = lax.rem(s + b, m)
        dev = {"ops": o, "sec": to}
        third.append(begin(remote(renorm.at[:, portion(to)], taken.at[b - 1], send3.at[b - 1], recv3.at[b - 1], dev)))

    def sum_and_spread():
        sector = renorm[:, ours, :]
        for b in range(1, m):
            third[b - 1].wait_recv()
            sector += taken[b - 1]
        merged[:, ours, :] = sector
        for b in range(1, m):
            dev = {"ops": o, "sec": lax.rem(s + b, m)}
            begin(remote(merged.at[:, ours], merged.at[:, ours], send5.at[b - 1], recv5.at[b - 1], dev))

    block = 64
    work[:, :cols] = whole[...]
    work[:, cols:] = (
        lax.broadcasted_iota(jnp.int32, (cols, cols), 0) == lax.broadcasted_iota(jnp.int32, (cols, cols), 1)
    ).astype(jnp.float32)
    for at in range(0, cols, block):
        end = at + block
        small = small_inverse(work[at:end, at:end])
        strip = dot(small, work[at:end, :], NN, HIGHEST)
        inverse[at:end, :] = strip[:, cols:]
        if end < cols:
            work[end:, :] -= dot(strip[:, end:cols], strip, TN, HIGHEST)
        if at == cols // 2 - block:
            sum_and_spread()
    for p in range(SITE):
        part = slice(p * cols, (p + 1) * cols)
        frame[:, part] = dot(x[:, part], inverse[...], NT, HIGH)

    basis_ref[...] = frame[pl.ds(pl.multiple_of(o * row_share, row_share), row_share), :] * scale

    for b in range(1, m):
        at = portion(lax.rem(s + m - b, m))
        dev = {"ops": o, "sec": lax.rem(s + b, m)}
        remote(merged.at[:, at], merged.at[:, at], send5.at[b - 1], recv5.at[b - 1], dev).wait_recv()
    for k in range(pairs):
        summed[0, k] = dot(dot(inverse[ours, :], merged[k], NN, HIGHEST), inverse[...], NT, HIGHEST)
    fourth = []
    for a in range(1, n):
        dev = {"ops": lax.rem(o + a, n), "sec": s}
        fourth.append(begin(remote(summed.at[0], summed.at[a], send4.at[a - 1], recv4.at[a - 1], dev)))
    result = [jnp.zeros((share, cols), jnp.float32) for _ in range(SLOTS)]
    base = (o * SLOTS).astype(jnp.float32)
    for a in range(n):
        if a:
            fourth[a - 1].wait_recv()
        at = lax.rem(o + n - a, n)
        for k in range(pairs):
            term = summed[a, k]
            target = scalar(at, k, SITE * SITE + 1) * SLOTS + scalar(at, k, SITE * SITE + 2) - base
            for j in range(SLOTS):
                result[j] += term * (target == j).astype(jnp.float32)
    for j in range(SLOTS):
        out_ref[j] = result[j]
    for c in pending:
        c.wait_send()


def body(n, m, wavefunction, left_ops, right_ops, site_ops, pattern, sector_sizes, owner, slot):
    row_share, width = wavefunction.shape[1:]
    pairs = left_ops.shape[0]
    cols = width // SITE
    states = row_share * n
    f32 = jnp.float32
    meta = jnp.concatenate(
        [
            site_ops.reshape(pairs, SITE * SITE),
            pattern[:, :1].astype(f32),
            owner[:, None].astype(f32),
            slot[:, None].astype(f32),
        ],
        axis=1,
    )
    meta = jnp.pad(meta, ((0, 0), (0, 128 - meta.shape[1])))
    wide = cols % (8 * n * m) == 0
    rows = cols // (n * m) if wide else cols // m
    share = cols // m
    dma = pltpu.SemaphoreType.DMA
    peers = n * m - 1
    basis, complementary = pl.pallas_call(
        functools.partial(kernel, n, m, wide, float(SITE * states * m) ** 0.5),
        out_shape=[
            jax.ShapeDtypeStruct((row_share, width), f32),
            jax.ShapeDtypeStruct((SLOTS, share, cols), f32),
        ],
        in_specs=[SM, VM, ANY, ANY, ANY],
        out_specs=[VM, VM],
        scratch_shapes=[
            pltpu.VMEM((n, pairs, 128), f32),
            pltpu.VMEM((n, row_share, width), f32),
            pltpu.VMEM((n, pairs, states, states), f32),
            pltpu.VMEM((n, pairs, cols, cols), f32),
            pltpu.VMEM((n * pairs, states, width), f32),
            pltpu.VMEM((states, width), f32),
            pltpu.VMEM((cols, cols), f32),
            pltpu.VMEM((cols, cols), f32),
            pltpu.VMEM((m - 1, rows, cols), f32),
            pltpu.VMEM((cols, 2 * cols), f32),
            pltpu.VMEM((cols, cols), f32),
            pltpu.VMEM((states, width), f32),
            pltpu.VMEM((pairs, cols, cols), f32),
            pltpu.VMEM((pairs, states, width), f32),
            pltpu.VMEM((pairs, cols, cols), f32),
            pltpu.VMEM((m - 1, pairs, share, cols), f32),
            pltpu.VMEM((n, pairs, share, cols), f32),
            dma((4, n)),
            dma((4, n)),
            dma((4,)),
            dma((m - 1,)),
            dma((m - 1,)),
            dma((peers,)),
            dma((peers,)),
            dma((m - 1,)),
            dma((m - 1,)),
            dma((n - 1,)),
            dma((n - 1,)),
            dma((m - 1,)),
            dma((m - 1,)),
        ],
        compiler_params=pltpu.CompilerParams(collective_id=0, has_side_effects=True, vmem_limit_bytes=LIMIT),
    )(sector_sizes, meta, wavefunction[0], left_ops[:, 0], right_ops)
    return basis[None], complementary[None]


def solution(mesh):
    placed = (
        P("sec", "ops", None),
        P("ops", "sec", None, None),
        P("ops", None, None),
        P("ops", None, None),
        P("ops", "sec"),
        P("sec"),
        P("ops"),
        P("ops"),
    )
    return jax.shard_map(
        functools.partial(body, mesh.shape["ops"], mesh.shape["sec"]),
        mesh=mesh,
        in_specs=placed,
        out_specs=(P("sec", "ops", None), P("ops", None, "sec", None)),
        check_vma=False,
    )
```

```python
import functools

import jax
import jax.numpy as jnp
from jax import lax
from jax.experimental import pallas as pl
from jax.experimental.pallas import tpu as pltpu
from jax.sharding import PartitionSpec as P

SLOTS = 2
SITE = 4
HIGHEST = lax.Precision.HIGHEST
HIGH = lax.Precision.HIGH
MESH = pl.DeviceIdType.MESH
VM = pl.BlockSpec(memory_space=pltpu.VMEM)
SM = pl.BlockSpec(memory_space=pltpu.SMEM)
ANY = pl.BlockSpec(memory_space=pl.ANY)
LIMIT = 60 * 1024 * 1024


def remote(src, dst, send, recv, dev):
    return pltpu.make_async_remote_copy(
        src_ref=src, dst_ref=dst, send_sem=send, recv_sem=recv, device_id=dev, device_id_type=MESH
    )


def greet(devs):
    barrier = pltpu.get_barrier_semaphore()
    for dev in devs:
        pl.semaphore_signal(barrier, inc=1, device_id=dev, device_id_type=MESH)
    pl.semaphore_wait(barrier, len(devs))


def dot(a, b, dims, precision):
    return lax.dot_general(a, b, (dims, ((), ())), precision=precision, preferred_element_type=jnp.float32)


NN = ((1,), (0,))
NT = ((1,), (1,))
TN = ((0,), (0,))


def small_inverse(block):
    b = block.shape[0]
    eye = (
        lax.broadcasted_iota(jnp.int32, (b, b), 0) == lax.broadcasted_iota(jnp.int32, (b, b), 1)
    ).astype(jnp.float32)
    work = jnp.concatenate([block, eye], axis=1)
    lanes = work.shape[1]
    count = b // 8
    parts = [work[t * 8:(t + 1) * 8] for t in range(count)]
    under = lax.broadcasted_iota(jnp.int32, (8, lanes), 0)
    for g in range(count):
        spread = [
            [jnp.broadcast_to(parts[t][:, g * 8 + i:g * 8 + i + 1], (8, lanes)) for i in range(8)]
            for t in range(g, count)
        ]
        rows = parts[g]
        for r in range(8):
            inv = 1.0 / spread[0][r][r:r + 1, :]
            ratio = rows[r:r + 1, :] * inv
            steps = [spread[0][i][r:r + 1, :] * inv for i in range(r + 1, 8)]
            for t in range(count - g):
                col = spread[t][r]
                if t == 0:
                    if r == 7:
                        continue
                    col = jnp.where(under > r, col, 0.0)
                    rows = rows - col * ratio
                else:
                    parts[g + t] = parts[g + t] - col * ratio
                for i in range(r + 1, 8):
                    spread[t][i] = spread[t][i] - col * steps[i - r - 1]
        parts[g] = rows
    work = jnp.concatenate(parts, axis=0)
    pivot = jnp.sum(work[:, :b] * eye, axis=1, keepdims=True)
    return work[:, b:] / jnp.sqrt(pivot)


def kernel(
    n, m, wide, size_ref, meta_in, psi_in, left_in, right_in, basis_ref, out_ref,
    meta, psi, left, right, mixed, x, gram, whole, held, work, inverse, frame, renorm, moved, merged, taken, summed,
    send, recv, local, send1, recv1, send2, recv2, send3, recv3, send4, recv4, send5, recv5, send6, recv6,
):
    o, s = lax.axis_index("ops"), lax.axis_index("sec")
    pairs = left_in.shape[0]
    row_share, width = psi_in.shape
    states = row_share * n
    cols = width // SITE
    others = [(a, b) for a in range(n) for b in range(m) if (a or b) and not (a and b)]
    devs = [{"ops": lax.rem(o + a, n), "sec": lax.rem(s + b, m)} for a, b in others]
    greet(devs)

    ins, outs = (meta_in, psi_in, right_in, left_in), (meta, psi, right, left)
    chips = n // 2
    core = lax.rem(o, 2)
    chip = o // 2
    direct = chips - 1
    mate_at = chip * 2 + 1 - core
    mate = {"ops": mate_at, "sec": s}
    away = [{"ops": lax.rem(chip + d, chips) * 2 + core, "sec": s} for d in range(1, chips)]
    back = [lax.rem(chip + chips - d, chips) * 2 + core for d in range(1, chips)]
    far = [lax.rem(chip + chips - d, chips) * 2 + 1 - core for d in range(1, chips)]
    side = lax.rem(s, 2)
    half = cols // 2
    ours_half = pl.ds(pl.multiple_of(side * half, half), half)
    other_half = pl.ds(pl.multiple_of((1 - side) * half, half), half)
    twin = {"ops": o, "sec": s + 1 - 2 * side}
    pending = []

    def begin(c):
        c.start()
        pending.append(c)
        return c

    own = [pltpu.make_async_copy(ins[a], outs[a].at[o], local.at[a]) for a in range(4)]
    for a in range(4):
        for i, dev in enumerate(away):
            if a == 2:
                begin(remote(right_in.at[:, ours_half], right.at[o, :, ours_half], send.at[a, i], recv.at[a, i], dev))
            else:
                begin(remote(ins[a], outs[a].at[o], send.at[a, i], recv.at[a, i], dev))
        begin(remote(ins[a], outs[a].at[o], send.at[a, direct], recv.at[a, direct], mate))
        own[a].start()

    def relay(a):
        for i, src in enumerate(back):
            remote(ins[a], outs[a].at[src], send.at[a, i], recv.at[a, i], away[i]).wait_recv()
            begin(remote(outs[a].at[src], outs[a].at[src], send.at[a, chips + i], recv.at[a, chips + i], mate))

    def relay_right():
        for i, src in enumerate(back):
            here = right.at[src, :, ours_half]
            remote(here, here, send.at[2, i], recv.at[2, i], away[i]).wait_recv()
            begin(remote(here, here, send6.at[i], recv6.at[i], twin))
            begin(remote(here, here, send.at[2, chips + i], recv.at[2, chips + i], mate))
        for i, src in enumerate(back):
            here = right.at[src, :, other_half]
            remote(here, here, send6.at[i], recv6.at[i], twin).wait_recv()
            begin(remote(here, here, send6.at[chips + i], recv6.at[chips + i], mate))

    def far_right(i):
        here = right.at[far[i], :, ours_half]
        remote(here, here, send.at[2, chips + i], recv.at[2, chips + i], mate).wait_recv()
        here = right.at[far[i], :, other_half]
        remote(here, here, send6.at[chips + i], recv6.at[chips + i], mate).wait_recv()

    def from_mate(a):
        remote(ins[a], outs[a].at[mate_at], send.at[a, direct], recv.at[a, direct], mate).wait_recv()

    def from_far(a, i):
        remote(outs[a].at[far[i]], outs[a].at[far[i]], send.at[a, chips + i], recv.at[a, chips + i], mate).wait_recv()

    for a in (0, 1):
        own[a].wait()
        from_mate(a)
        relay(a)
        for i in range(direct):
            from_far(a, i)

    live = lax.broadcasted_iota(jnp.int32, (states, width), 0) < size_ref[0]
    x[...] = jnp.where(live, psi[...].reshape(states, width), 0.0)
    order = [o, mate_at] + back + far

    def scalar(at, k, i):
        return meta[at, k:k + 1, i:i + 1]

    def mix_site(parts, at, k, p):
        total = parts[0] * scalar(at, k, p * SITE)
        for q in range(1, SITE):
            total += parts[q] * scalar(at, k, p * SITE + q)
        return total

    def map_right(i):
        for k in range(pairs):
            mapped = [
                dot(x[:, q * cols:(q + 1) * cols], right[order[i], k], NN, HIGH) for q in range(SITE)
            ]
            for p in range(SITE):
                mixed[i * pairs + k, :, p * cols:(p + 1) * cols] = mix_site(mapped, order[i], k, p)

    def apply_left(i, total):
        for k in range(pairs):
            block = left[order[i], k] * scalar(order[i], k, SITE * SITE)
            total = total + dot(block, mixed[i * pairs + k], NN, HIGH)
        return total

    def arrive(a, i):
        if i == 0:
            own[a].wait()
        elif i == 1:
            from_mate(a)
        elif i < 2 + direct:
            if i == 2:
                relay_right() if a == 2 else relay(a)
        elif a == 2:
            far_right(i - 2 - direct)
        else:
            from_far(a, i - 2 - direct)

    for i in range(n):
        arrive(2, i)
        map_right(i)
    total = jnp.zeros((states, width), jnp.float32)
    for i in range(n):
        arrive(3, i)
        total = apply_left(i, total)
    x[...] = jnp.where(live, total, 0.0)
    gram[...] = sum(dot(x[:, p * cols:(p + 1) * cols], x[:, p * cols:(p + 1) * cols], TN, HIGH) for p in range(SITE))

    rows = held.shape[1]

    def place(a, b):
        at = a * m + b if wide else b
        return pl.ds(pl.multiple_of(at * rows, rows), rows)

    first = []
    for b in range(1, m):
        to = lax.rem(s + b, m)
        dev = {"ops": o, "sec": to}
        first.append(begin(remote(gram.at[place(o, to)], held.at[b - 1], send1.at[b - 1], recv1.at[b - 1], dev)))
    for k in range(pairs):
        moved[k] = dot(left[o, k] * scalar(o, k, SITE * SITE), x[...], NN, HIGHEST)
    mine = place(o, s)
    part = gram[mine, :]
    for b in range(1, m):
        first[b - 1].wait_recv()
        part += held[b - 1]
    whole[mine, :] = part
    for b in range(1, m):
        dev = {"ops": o, "sec": lax.rem(s + b, m)}
        begin(remote(whole.at[mine], whole.at[mine], send2.at[b - 1], recv2.at[b - 1], dev))
    for b in range(m):
        at = place(o, lax.rem(s + m - b, m))
        if b:
            dev = {"ops": o, "sec": lax.rem(s + b, m)}
            remote(whole.at[at], whole.at[at], send2.at[b - 1], recv2.at[b - 1], dev).wait_recv()
        for a in range(1, n if wide else 1):
            i = a * m - 1 + b
            dev = {"ops": lax.rem(o + a, n), "sec": s}
            begin(remote(whole.at[at], whole.at[at], send2.at[i], recv2.at[i], dev))
    for k in range(pairs):
        parts = [moved[k, :, q * cols:(q + 1) * cols] for q in range(SITE)]
        renorm[k] = sum(
            dot(x[:, p * cols:(p + 1) * cols], mix_site(parts, o, k, p), TN, HIGHEST) for p in range(SITE)
        )

    share = taken.shape[2]

    def portion(b):
        return pl.ds(pl.multiple_of(b * share, share), share)

    ours = portion(s)
    third = []
    for b in range(1, m):
        to = lax.rem(s + b, m)
        dev = {"ops": o, "sec": to}
        third.append(begin(remote(renorm.at[:, portion(to)], taken.at[b - 1], send3.at[b - 1], recv3.at[b - 1], dev)))
    for a in range(1, n if wide else 1):
        for b in range(m):
            i = a * m - 1 + b
            at = place(lax.rem(o + n - a, n), lax.rem(s + m - b, m))
            dev = {"ops": lax.rem(o + a, n), "sec": s}
            remote(whole.at[at], whole.at[at], send2.at[i], recv2.at[i], dev).wait_recv()

    def sum_and_spread():
        sector = renorm[:, ours, :]
        for b in range(1, m):
            third[b - 1].wait_recv()
            sector += taken[b - 1]
        merged[:, ours, :] = sector
        for b in range(1, m):
            dev = {"ops": o, "sec": lax.rem(s + b, m)}
            begin(remote(merged.at[:, ours], merged.at[:, ours], send5.at[b - 1], recv5.at[b - 1], dev))

    block = 64
    work[:, :cols] = whole[...]
    work[:, cols:] = (
        lax.broadcasted_iota(jnp.int32, (cols, cols), 0) == lax.broadcasted_iota(jnp.int32, (cols, cols), 1)
    ).astype(jnp.float32)
    for at in range(0, cols, block):
        end = at + block
        small = small_inverse(work[at:end, at:end])
        strip = dot(small, work[at:end, :], NN, HIGHEST)
        inverse[at:end, :] = strip[:, cols:]
        if end < cols:
            work[end:, :] -= dot(strip[:, end:cols], strip, TN, HIGH)
        if at == cols // 2 - block:
            sum_and_spread()
    for p in range(SITE):
        part = slice(p * cols, (p + 1) * cols)
        frame[:, part] = dot(x[:, part], inverse[...], NT, HIGH)

    basis_ref[...] = frame[pl.ds(pl.multiple_of(o * row_share, row_share), row_share), :]

    for b in range(1, m):
        at = portion(lax.rem(s + m - b, m))
        dev = {"ops": o, "sec": lax.rem(s + b, m)}
        remote(merged.at[:, at], merged.at[:, at], send5.at[b - 1], recv5.at[b - 1], dev).wait_recv()
    for k in range(pairs):
        summed[0, k] = dot(dot(inverse[ours, :], merged[k], NN, HIGHEST), inverse[...], NT, HIGHEST)
    fourth = []
    for a in range(1, n):
        dev = {"ops": lax.rem(o + a, n), "sec": s}
        fourth.append(begin(remote(summed.at[0], summed.at[a], send4.at[a - 1], recv4.at[a - 1], dev)))
    result = [jnp.zeros((share, cols), jnp.float32) for _ in range(SLOTS)]
    base = (o * SLOTS).astype(jnp.float32)
    for a in range(n):
        if a:
            fourth[a - 1].wait_recv()
        at = lax.rem(o + n - a, n)
        for k in range(pairs):
            term = summed[a, k]
            target = scalar(at, k, SITE * SITE + 1) * SLOTS + scalar(at, k, SITE * SITE + 2) - base
            for j in range(SLOTS):
                result[j] += term * (target == j).astype(jnp.float32)
    for j in range(SLOTS):
        out_ref[j] = result[j]
    for c in pending:
        c.wait_send()


def body(n, m, wavefunction, left_ops, right_ops, site_ops, pattern, sector_sizes, owner, slot):
    row_share, width = wavefunction.shape[1:]
    pairs = left_ops.shape[0]
    cols = width // SITE
    states = row_share * n
    f32 = jnp.float32
    meta = jnp.concatenate(
        [
            site_ops.reshape(pairs, SITE * SITE),
            pattern[:, :1].astype(f32),
            owner[:, None].astype(f32),
            slot[:, None].astype(f32),
        ],
        axis=1,
    )
    meta = jnp.pad(meta, ((0, 0), (0, 128 - meta.shape[1])))
    wide = cols % (8 * n * m) == 0
    rows = cols // (n * m) if wide else cols // m
    share = cols // m
    dma = pltpu.SemaphoreType.DMA
    peers = n * m - 1
    basis, complementary = pl.pallas_call(
        functools.partial(kernel, n, m, wide),
        out_shape=[
            jax.ShapeDtypeStruct((row_share, width), f32),
            jax.ShapeDtypeStruct((SLOTS, share, cols), f32),
        ],
        in_specs=[SM, VM, ANY, ANY, ANY],
        out_specs=[VM, VM],
        scratch_shapes=[
            pltpu.VMEM((n, pairs, 128), f32),
            pltpu.VMEM((n, row_share, width), f32),
            pltpu.VMEM((n, pairs, states, states), f32),
            pltpu.VMEM((n, pairs, cols, cols), f32),
            pltpu.VMEM((n * pairs, states, width), f32),
            pltpu.VMEM((states, width), f32),
            pltpu.VMEM((cols, cols), f32),
            pltpu.VMEM((cols, cols), f32),
            pltpu.VMEM((m - 1, rows, cols), f32),
            pltpu.VMEM((cols, 2 * cols), f32),
            pltpu.VMEM((cols, cols), f32),
            pltpu.VMEM((states, width), f32),
            pltpu.VMEM((pairs, cols, cols), f32),
            pltpu.VMEM((pairs, states, width), f32),
            pltpu.VMEM((pairs, cols, cols), f32),
            pltpu.VMEM((m - 1, pairs, share, cols), f32),
            pltpu.VMEM((n, pairs, share, cols), f32),
            dma((4, n)),
            dma((4, n)),
            dma((4,)),
            dma((m - 1,)),
            dma((m - 1,)),
            dma((peers,)),
            dma((peers,)),
            dma((m - 1,)),
            dma((m - 1,)),
            dma((n - 1,)),
            dma((n - 1,)),
            dma((m - 1,)),
            dma((m - 1,)),
            dma((n,)),
            dma((n,)),
        ],
        compiler_params=pltpu.CompilerParams(collective_id=0, has_side_effects=True, vmem_limit_bytes=LIMIT),
    )(sector_sizes, meta, wavefunction[0], left_ops[:, 0], right_ops)
    return (basis * (float(SITE * states * m) ** 0.5))[None], complementary[None]


def solution(mesh):
    placed = (
        P("sec", "ops", None),
        P("ops", "sec", None, None),
        P("ops", None, None),
        P("ops", None, None),
        P("ops", "sec"),
        P("sec"),
        P("ops"),
        P("ops"),
    )
    return jax.shard_map(
        functools.partial(body, mesh.shape["ops"], mesh.shape["sec"]),
        mesh=mesh,
        in_specs=placed,
        out_specs=(P("sec", "ops", None), P("ops", None, "sec", None)),
        check_vma=False,
    )
```

```python
import functools

import jax
import jax.numpy as jnp
from jax import lax
from jax.experimental import pallas as pl
from jax.experimental.pallas import tpu as pltpu
from jax.sharding import PartitionSpec as P

SLOTS = 2
SITE = 4
HIGHEST = lax.Precision.HIGHEST
HIGH = lax.Precision.HIGH
MESH = pl.DeviceIdType.MESH
VM = pl.BlockSpec(memory_space=pltpu.VMEM)
SM = pl.BlockSpec(memory_space=pltpu.SMEM)
ANY = pl.BlockSpec(memory_space=pl.ANY)
LIMIT = 60 * 1024 * 1024


def remote(src, dst, send, recv, dev):
    return pltpu.make_async_remote_copy(
        src_ref=src, dst_ref=dst, send_sem=send, recv_sem=recv, device_id=dev, device_id_type=MESH
    )


def greet(devs):
    barrier = pltpu.get_barrier_semaphore()
    for dev in devs:
        pl.semaphore_signal(barrier, inc=1, device_id=dev, device_id_type=MESH)
    pl.semaphore_wait(barrier, len(devs))


def dot(a, b, dims, precision):
    return lax.dot_general(a, b, (dims, ((), ())), precision=precision, preferred_element_type=jnp.float32)


NN = ((1,), (0,))
NT = ((1,), (1,))
TN = ((0,), (0,))


def small_inverse(block):
    b = block.shape[0]
    eye = (
        lax.broadcasted_iota(jnp.int32, (b, b), 0) == lax.broadcasted_iota(jnp.int32, (b, b), 1)
    ).astype(jnp.float32)
    work = jnp.concatenate([block, eye], axis=1)
    lanes = work.shape[1]
    count = b // 8
    parts = [work[t * 8:(t + 1) * 8] for t in range(count)]
    under = lax.broadcasted_iota(jnp.int32, (8, lanes), 0)
    for g in range(count):
        spread = [
            [jnp.broadcast_to(parts[t][:, g * 8 + i:g * 8 + i + 1], (8, lanes)) for i in range(8)]
            for t in range(g, count)
        ]
        rows = parts[g]
        for r in range(8):
            pivot = spread[0][r][r:r + 1, :]
            inv = pl.reciprocal(pivot, approx=True)
            inv = inv * (2.0 - pivot * inv)
            inv = inv * (2.0 - pivot * inv)
            ratio = rows[r:r + 1, :] * inv
            above = [spread[0][i][r:r + 1, :] for i in range(r + 1, 8)]
            steps = [a * inv for a in above]
            for t in range(count - g):
                col = spread[t][r]
                if t == 0:
                    if r == 7:
                        continue
                    col = jnp.where(under > r, col, 0.0)
                    rows = rows - col * ratio
                else:
                    parts[g + t] = parts[g + t] - col * ratio
                for i in range(r + 1, 8):
                    if t == 0:
                        spread[t][i] = spread[t][i] - (col * above[i - r - 1]) * inv
                    else:
                        spread[t][i] = spread[t][i] - col * steps[i - r - 1]
        parts[g] = rows
    work = jnp.concatenate(parts, axis=0)
    pivot = jnp.sum(work[:, :b] * eye, axis=1, keepdims=True)
    return work[:, b:] / jnp.sqrt(pivot)


def kernel(
    n, m, wide, size_ref, meta_in, psi_in, left_in, right_in, basis_ref, out_ref,
    meta, psi, left, right, mixed, x, gram, whole, held, work, inverse, frame, renorm, moved, merged, taken, summed,
    send, recv, local, send1, recv1, send2, recv2, send3, recv3, send4, recv4, send5, recv5, send6, recv6,
):
    o, s = lax.axis_index("ops"), lax.axis_index("sec")
    pairs = left_in.shape[0]
    row_share, width = psi_in.shape
    states = row_share * n
    cols = width // SITE
    others = [(a, b) for a in range(n) for b in range(m) if (a or b) and not (a and b)]
    devs = [{"ops": lax.rem(o + a, n), "sec": lax.rem(s + b, m)} for a, b in others]
    greet(devs)

    ins, outs = (meta_in, psi_in, right_in, left_in), (meta, psi, right, left)
    chips = n // 2
    core = lax.rem(o, 2)
    chip = o // 2
    direct = chips - 1
    mate_at = chip * 2 + 1 - core
    mate = {"ops": mate_at, "sec": s}
    away = [{"ops": lax.rem(chip + d, chips) * 2 + core, "sec": s} for d in range(1, chips)]
    back = [lax.rem(chip + chips - d, chips) * 2 + core for d in range(1, chips)]
    far = [lax.rem(chip + chips - d, chips) * 2 + 1 - core for d in range(1, chips)]
    side = lax.rem(s, 2)
    half = cols // 2
    ours_half = pl.ds(pl.multiple_of(side * half, half), half)
    other_half = pl.ds(pl.multiple_of((1 - side) * half, half), half)
    twin = {"ops": o, "sec": s + 1 - 2 * side}
    pending = []

    def begin(c):
        c.start()
        pending.append(c)
        return c

    own = [pltpu.make_async_copy(ins[a], outs[a].at[o], local.at[a]) for a in range(4)]
    for a in range(4):
        for i, dev in enumerate(away):
            if a == 2:
                begin(remote(right_in.at[:, ours_half], right.at[o, :, ours_half], send.at[a, i], recv.at[a, i], dev))
            else:
                begin(remote(ins[a], outs[a].at[o], send.at[a, i], recv.at[a, i], dev))
        begin(remote(ins[a], outs[a].at[o], send.at[a, direct], recv.at[a, direct], mate))
        own[a].start()

    def relay(a):
        for i, src in enumerate(back):
            remote(ins[a], outs[a].at[src], send.at[a, i], recv.at[a, i], away[i]).wait_recv()
            begin(remote(outs[a].at[src], outs[a].at[src], send.at[a, chips + i], recv.at[a, chips + i], mate))

    def relay_right():
        for i, src in enumerate(back):
            here = right.at[src, :, ours_half]
            remote(here, here, send.at[2, i], recv.at[2, i], away[i]).wait_recv()
            begin(remote(here, here, send6.at[i], recv6.at[i], twin))
            begin(remote(here, here, send.at[2, chips + i], recv.at[2, chips + i], mate))
        for i, src in enumerate(back):
            here = right.at[src, :, other_half]
            remote(here, here, send6.at[i], recv6.at[i], twin).wait_recv()
            begin(remote(here, here, send6.at[chips + i], recv6.at[chips + i], mate))

    def far_right(i):
        here = right.at[far[i], :, ours_half]
        remote(here, here, send.at[2, chips + i], recv.at[2, chips + i], mate).wait_recv()
        here = right.at[far[i], :, other_half]
        remote(here, here, send6.at[chips + i], recv6.at[chips + i], mate).wait_recv()

    def from_mate(a):
        remote(ins[a], outs[a].at[mate_at], send.at[a, direct], recv.at[a, direct], mate).wait_recv()

    def from_far(a, i):
        remote(outs[a].at[far[i]], outs[a].at[far[i]], send.at[a, chips + i], recv.at[a, chips + i], mate).wait_recv()

    for a in (0, 1):
        own[a].wait()
        from_mate(a)
        relay(a)
        for i in range(direct):
            from_far(a, i)

    live = lax.broadcasted_iota(jnp.int32, (states, width), 0) < size_ref[0]
    x[...] = jnp.where(live, psi[...].reshape(states, width), 0.0)
    order = [o, mate_at] + back + far

    def scalar(at, k, i):
        return meta[at, k:k + 1, i:i + 1]

    def mix_site(parts, at, k, p):
        total = parts[0] * scalar(at, k, p * SITE)
        for q in range(1, SITE):
            total += parts[q] * scalar(at, k, p * SITE + q)
        return total

    def map_right(i):
        for k in range(pairs):
            mapped = [
                dot(x[:, q * cols:(q + 1) * cols], right[order[i], k], NN, HIGH) for q in range(SITE)
            ]
            for p in range(SITE):
                mixed[i * pairs + k, :, p * cols:(p + 1) * cols] = mix_site(mapped, order[i], k, p)

    def apply_left(i, total):
        for k in range(pairs):
            block = left[order[i], k] * scalar(order[i], k, SITE * SITE)
            total = total + dot(block, mixed[i * pairs + k], NN, HIGH)
        return total

    def arrive(a, i):
        if i == 0:
            own[a].wait()
        elif i == 1:
            from_mate(a)
        elif i < 2 + direct:
            if i == 2:
                relay_right() if a == 2 else relay(a)
        elif a == 2:
            far_right(i - 2 - direct)
        else:
            from_far(a, i - 2 - direct)

    for i in range(n):
        arrive(2, i)
        map_right(i)
    total = jnp.zeros((states, width), jnp.float32)
    for i in range(n):
        arrive(3, i)
        total = apply_left(i, total)
    x[...] = jnp.where(live, total, 0.0)
    gram[...] = sum(dot(x[:, p * cols:(p + 1) * cols], x[:, p * cols:(p + 1) * cols], TN, HIGH) for p in range(SITE))

    rows = held.shape[1]

    def place(a, b):
        at = a * m + b if wide else b
        return pl.ds(pl.multiple_of(at * rows, rows), rows)

    first = []
    for b in range(1, m):
        to = lax.rem(s + b, m)
        dev = {"ops": o, "sec": to}
        first.append(begin(remote(gram.at[place(o, to)], held.at[b - 1], send1.at[b - 1], recv1.at[b - 1], dev)))
    for k in range(pairs):
        moved[k] = dot(left[o, k] * scalar(o, k, SITE * SITE), x[...], NN, HIGHEST)
    mine = place(o, s)
    part = gram[mine, :]
    for b in range(1, m):
        first[b - 1].wait_recv()
        part += held[b - 1]
    whole[mine, :] = part
    for b in range(1, m):
        dev = {"ops": o, "sec": lax.rem(s + b, m)}
        begin(remote(whole.at[mine], whole.at[mine], send2.at[b - 1], recv2.at[b - 1], dev))
    for b in range(m):
        at = place(o, lax.rem(s + m - b, m))
        if b:
            dev = {"ops": o, "sec": lax.rem(s + b, m)}
            remote(whole.at[at], whole.at[at], send2.at[b - 1], recv2.at[b - 1], dev).wait_recv()
        for a in range(1, n if wide else 1):
            i = a * m - 1 + b
            dev = {"ops": lax.rem(o + a, n), "sec": s}
            begin(remote(whole.at[at], whole.at[at], send2.at[i], recv2.at[i], dev))
    for k in range(pairs):
        parts = [moved[k, :, q * cols:(q + 1) * cols] for q in range(SITE)]
        renorm[k] = sum(
            dot(x[:, p * cols:(p + 1) * cols], mix_site(parts, o, k, p), TN, HIGHEST) for p in range(SITE)
        )

    share = taken.shape[2]

    def portion(b):
        return pl.ds(pl.multiple_of(b * share, share), share)

    ours = portion(s)
    third = []
    for b in range(1, m):
        to = lax.rem(s + b, m)
        dev = {"ops": o, "sec": to}
        third.append(begin(remote(renorm.at[:, portion(to)], taken.at[b - 1], send3.at[b - 1], recv3.at[b - 1], dev)))
    for a in range(1, n if wide else 1):
        for b in range(m):
            i = a * m - 1 + b
            at = place(lax.rem(o + n - a, n), lax.rem(s + m - b, m))
            dev = {"ops": lax.rem(o + a, n), "sec": s}
            remote(whole.at[at], whole.at[at], send2.at[i], recv2.at[i], dev).wait_recv()

    def sum_and_spread():
        sector = renorm[:, ours, :]
        for b in range(1, m):
            third[b - 1].wait_recv()
            sector += taken[b - 1]
        merged[:, ours, :] = sector
        for b in range(1, m):
            dev = {"ops": o, "sec": lax.rem(s + b, m)}
            begin(remote(merged.at[:, ours], merged.at[:, ours], send5.at[b - 1], recv5.at[b - 1], dev))

    block = 64
    work[:, :cols] = whole[...]
    work[:, cols:] = (
        lax.broadcasted_iota(jnp.int32, (cols, cols), 0) == lax.broadcasted_iota(jnp.int32, (cols, cols), 1)
    ).astype(jnp.float32)
    for at in range(0, cols, block):
        end = at + block
        small = small_inverse(work[at:end, at:end])
        strip = dot(small, work[at:end, :], NN, HIGHEST)
        inverse[at:end, :] = strip[:, cols:]
        if end < cols:
            work[end:, :] -= dot(strip[:, end:cols], strip, TN, HIGH)
        if at == cols // 2 - block:
            sum_and_spread()
    for p in range(SITE):
        part = slice(p * cols, (p + 1) * cols)
        frame[:, part] = dot(x[:, part], inverse[...], NT, HIGH)

    basis_ref[...] = frame[pl.ds(pl.multiple_of(o * row_share, row_share), row_share), :]

    for b in range(1, m):
        at = portion(lax.rem(s + m - b, m))
        dev = {"ops": o, "sec": lax.rem(s + b, m)}
        remote(merged.at[:, at], merged.at[:, at], send5.at[b - 1], recv5.at[b - 1], dev).wait_recv()
    for k in range(pairs):
        summed[0, k] = dot(dot(inverse[ours, :], merged[k], NN, HIGHEST), inverse[...], NT, HIGHEST)
    fourth = []
    for a in range(1, n):
        dev = {"ops": lax.rem(o + a, n), "sec": s}
        fourth.append(begin(remote(summed.at[0], summed.at[a], send4.at[a - 1], recv4.at[a - 1], dev)))
    result = [jnp.zeros((share, cols), jnp.float32) for _ in range(SLOTS)]
    base = (o * SLOTS).astype(jnp.float32)
    for a in range(n):
        if a:
            fourth[a - 1].wait_recv()
        at = lax.rem(o + n - a, n)
        for k in range(pairs):
            term = summed[a, k]
            target = scalar(at, k, SITE * SITE + 1) * SLOTS + scalar(at, k, SITE * SITE + 2) - base
            for j in range(SLOTS):
                result[j] += term * (target == j).astype(jnp.float32)
    for j in range(SLOTS):
        out_ref[j] = result[j]
    for c in pending:
        c.wait_send()


def body(n, m, wavefunction, left_ops, right_ops, site_ops, pattern, sector_sizes, owner, slot):
    row_share, width = wavefunction.shape[1:]
    pairs = left_ops.shape[0]
    cols = width // SITE
    states = row_share * n
    f32 = jnp.float32
    meta = jnp.concatenate(
        [
            site_ops.reshape(pairs, SITE * SITE),
            pattern[:, :1].astype(f32),
            owner[:, None].astype(f32),
            slot[:, None].astype(f32),
        ],
        axis=1,
    )
    meta = jnp.pad(meta, ((0, 0), (0, 128 - meta.shape[1])))
    wide = cols % (8 * n * m) == 0
    rows = cols // (n * m) if wide else cols // m
    share = cols // m
    dma = pltpu.SemaphoreType.DMA
    peers = n * m - 1
    basis, complementary = pl.pallas_call(
        functools.partial(kernel, n, m, wide),
        out_shape=[
            jax.ShapeDtypeStruct((row_share, width), f32),
            jax.ShapeDtypeStruct((SLOTS, share, cols), f32),
        ],
        in_specs=[SM, VM, ANY, ANY, ANY],
        out_specs=[VM, VM],
        scratch_shapes=[
            pltpu.VMEM((n, pairs, 128), f32),
            pltpu.VMEM((n, row_share, width), f32),
            pltpu.VMEM((n, pairs, states, states), f32),
            pltpu.VMEM((n, pairs, cols, cols), f32),
            pltpu.VMEM((n * pairs, states, width), f32),
            pltpu.VMEM((states, width), f32),
            pltpu.VMEM((cols, cols), f32),
            pltpu.VMEM((cols, cols), f32),
            pltpu.VMEM((m - 1, rows, cols), f32),
            pltpu.VMEM((cols, 2 * cols), f32),
            pltpu.VMEM((cols, cols), f32),
            pltpu.VMEM((states, width), f32),
            pltpu.VMEM((pairs, cols, cols), f32),
            pltpu.VMEM((pairs, states, width), f32),
            pltpu.VMEM((pairs, cols, cols), f32),
            pltpu.VMEM((m - 1, pairs, share, cols), f32),
            pltpu.VMEM((n, pairs, share, cols), f32),
            dma((4, n)),
            dma((4, n)),
            dma((4,)),
            dma((m - 1,)),
            dma((m - 1,)),
            dma((peers,)),
            dma((peers,)),
            dma((m - 1,)),
            dma((m - 1,)),
            dma((n - 1,)),
            dma((n - 1,)),
            dma((m - 1,)),
            dma((m - 1,)),
            dma((n,)),
            dma((n,)),
        ],
        compiler_params=pltpu.CompilerParams(collective_id=0, has_side_effects=True, vmem_limit_bytes=LIMIT),
    )(sector_sizes, meta, wavefunction[0], left_ops[:, 0], right_ops)
    return (basis * (float(SITE * states * m) ** 0.5))[None], complementary[None]


def solution(mesh):
    placed = (
        P("sec", "ops", None),
        P("ops", "sec", None, None),
        P("ops", None, None),
        P("ops", None, None),
        P("ops", "sec"),
        P("sec"),
        P("ops"),
        P("ops"),
    )
    return jax.shard_map(
        functools.partial(body, mesh.shape["ops"], mesh.shape["sec"]),
        mesh=mesh,
        in_specs=placed,
        out_specs=(P("sec", "ops", None), P("ops", None, "sec", None)),
        check_vma=False,
    )
```
